256 devices in a mesh: fsdp: 64 (over z_lo, x, y), tp: 4 (over z_hi, core).
Axes of the slice: x: 4, y: 4, z: 8 (z_hi: 2, z_lo: 4; z = z_hi * 4 + z_lo), core: 2. Of those that a mesh axis runs over, the one named last changes fastest.
Arguments:
- grad_out: bfloat16 [16384, 4096], P('fsdp', 'tp'), may hold values from -16 to 16
- gate_pre: bfloat16 [16384, 14336], P('fsdp', 'tp'), may hold values from -6 to 6
- up_pre: bfloat16 [16384, 14336], P('fsdp', 'tp'), may hold values from -1.5 to 1.5
- down_weight: bfloat16 [4096, 14336], P('fsdp', 'tp'), may hold values from -0.046875 to 0.046875
Outputs:
- grad_gate: bfloat16 [16384, 14336], P('fsdp', 'tp')
- grad_up: bfloat16 [16384, 14336], P('fsdp', 'tp')
- grad_down: bfloat16 [4096, 14336], P('fsdp', 'tp')
The draws below stay inside these ranges and needn't reach their ends.
All inputs are finite; a program needn't handle non-finite values.
Results may differ from the reference program's by a relative error of at most 0.0049.
Values may be sent and summed in bfloat16 or wider, within the bound.
A program may use at most 320 MiB of HBM per device.

```python
import jax
import jax.numpy as jnp
from jax import lax

D = 4096
FF = 14336
TOKENS = 16384


def with_spikes(values, key, source, target, shards_of, factor):
    owner, partner = [(jnp.arange(values.shape[axis_at]) // (values.shape[axis_at] // shards_of)).reshape([-1 if axis == axis_at else 1 for axis in range(values.ndim)]) for axis_at in (source, target)]
    chosen = jax.random.permutation(key, shards_of)[partner]
    strong = (owner == chosen) | (owner == (partner + shards_of // 2) % shards_of)
    return jnp.where(strong, factor * values, values)


def shard_levels(key, shape, shards, smallest, top_value):
    def one(position, blocks):
        draws = jax.random.uniform(jax.random.fold_in(jax.random.fold_in(key, 6), position), (blocks,), jnp.float32, smallest / len(shards), top_value / len(shards))
        return jnp.repeat(jnp.exp(draws), shape[position] // blocks).reshape((-1,) + (1,) * (len(shape) - position - 1))

    loudness = one(*shards[0])
    for cut in shards[1:]:
        loudness = loudness * one(*cut)
    return loudness


def bell_draw(stream_key, extent, deviation, bound, cuts=(), dtype=jnp.bfloat16):
    entries = jax.random.normal(stream_key, extent, jnp.float32) * deviation
    if len(cuts) > 0:
        entries = shard_levels(stream_key, extent, cuts, -0.22, 0.18) * entries
    return jnp.clip(entries, min=-bound, max=bound).astype(dtype)


def heavy_noise(stream_key, shape, deviation, limit, cuts, heavy, held_as=jnp.bfloat16):
    drawn = deviation * jax.random.normal(stream_key, shape, jnp.float32)
    if cuts:
        drawn = drawn * shard_levels(stream_key, shape, cuts, -0.22, 0.18)
    return jnp.clip(with_spikes(drawn, jax.random.fold_in(stream_key, 3), *heavy), -limit, limit).astype(held_as)


def setup_inputs(seed: int = 0) -> dict:
    arg_keys = jax.random.split(jax.random.key(seed), 5)
    return {
        "grad_out": heavy_noise(arg_keys[0], (TOKENS, D), 1.0, 16.0, ((0, 64), (1, 4)), (0, 1, 64, 4.0)),
        "gate_pre": bell_draw(arg_keys[1], (TOKENS, FF), 1.0, 6.0, ((0, 64), (1, 4))),
        "up_pre": bell_draw(arg_keys[2], (TOKENS, FF), 0.25, 1.5, ((0, 64), (1, 4))),
        "down_weight": bell_draw(arg_keys[3], (D, FF), FF ** -0.5, 0.046875, ((0, 64), (1, 4))),
    }


def reference(grad_out, gate_pre, up_pre, down_weight):
    gate_val = gate_pre.astype(jnp.float32)
    up_val = up_pre.astype(jnp.float32)
    sigmoid_gate = jax.nn.sigmoid(gate_val)
    swish_gate = gate_val * sigmoid_gate
    hidden = (swish_gate * up_val).astype(jnp.bfloat16)
    grad_hidden = jnp.dot(grad_out, down_weight, preferred_element_type=jnp.float32)
    grad_gate = (grad_hidden * up_val * sigmoid_gate * (1.0 + gate_val * (1.0 - sigmoid_gate))).astype(jnp.bfloat16)
    grad_up = (grad_hidden * swish_gate).astype(jnp.bfloat16)
    grad_down = lax.dot_general(grad_out, hidden, (((0,), (0,)), ((), ())), preferred_element_type=jnp.float32)
    return grad_gate, grad_up, grad_down.astype(jnp.bfloat16)
```

```python
import functools

import jax
import jax.numpy as jnp
from jax import lax
from jax.experimental import pallas as pl
from jax.experimental.pallas import tpu as pltpu
from jax.sharding import Mesh, PartitionSpec as P

AXES = ("zl", "x", "y", "zh", "c")
BF = jnp.bfloat16
F32 = jnp.float32


def dot(a, b):
    return lax.dot_general(a, b, (((1,), (0,)), ((), ())), preferred_element_type=F32)


def kernel(
    T, D, FB, DB,
    go_in, gate_in, up_in, w_in,
    gg_out, gu_out, gd_out,
    go, w, gate, up, ht, gh, ggs, gus, acc,
    far_s, far_r, near_s, near_r, z_s, z_r, fin,
    ssem, rsem, lsem,
):
    zl, x, y, zh, c = (lax.axis_index(a) for a in AXES)
    half_t, half_f, half_d = T // 2, FB // 2, DB // 2
    rows_w = DB // 4

    def al(v, m):
        return pl.multiple_of(v, m)

    def at(dz=0, dx=0, dy=0, dh=0, dc=0):
        return ((zl + dz) % 4, (x + dx) % 4, (y + dy) % 4, (zh + dh) % 2, (c + dc) % 2)

    ids = {}
    sends = []

    def rcopy(key, src, dst, dev, sem=None):
        i = ids.setdefault(key, len(ids)) if sem is None else sem
        cp = pltpu.make_async_remote_copy(
            src_ref=src, dst_ref=dst, send_sem=ssem.at[i], recv_sem=rsem.at[i],
            device_id=dev, device_id_type=pl.DeviceIdType.MESH,
        )
        return cp

    def send(key, src, dst, dev):
        cp = rcopy(key, src, dst, dev)
        cp.start()
        sends.append(cp)
        return cp

    nloc = [0]

    def lcopy(src, dst):
        cp = pltpu.make_async_copy(src, dst, lsem.at[nloc[0]])
        nloc[0] += 1
        cp.start()
        return cp

    partners = [at(dy=1), at(dy=2), at(dy=3), at(dx=1), at(dx=3),
                at(dz=1), at(dz=2), at(dz=3), at(dh=1), at(dc=1)]
    bar = pltpu.get_barrier_semaphore()
    for p in partners:
        pl.semaphore_signal(bar, inc=1, device_id=p, device_id_type=pl.DeviceIdType.MESH)
    pl.semaphore_wait(bar, len(partners))

    def fcols(yy):
        return pl.ds(al((yy % 4) * FB, 128), FB)

    def wrows(zz, xx, off=0, n=None):
        return pl.ds(al(((zz % 4) * 4 + xx % 4) * DB + off, 16), DB if n is None else n)

    def trows(yy, off=0, n=None):
        return pl.ds(al((yy % 4) * T + off, 16), T if n is None else n)

    my_w = pl.ds(al(((zl * 4 + x) * 4 + y) * rows_w, 16), rows_w)
    wy = [send(("wy", j), w_in.at[:, fcols(y + j)], w.at[my_w, :], at(dy=j)) for j in (1, 3, 2)]
    wl = lcopy(w_in.at[:, fcols(y)], w.at[my_w, :])

    def quarter(s):
        return 2 * ((zh + s % 2) % 2) + (c + s // 2) % 2

    def gblock(s, dy, off=0, n=None):
        return go.at[trows(y + dy, off, n), pl.ds(al(quarter(s) * D, 128), D)]

    gl = lcopy(go_in, gblock(0, 0))
    gz = send("gz", go_in, gblock(0, 0), at(dh=1))
    gc00 = send(("gc", 0, 0), go_in, gblock(0, 0), at(dc=1))
    gu = {}
    for j in (1, 3, 2):
        gu[j] = (
            send(("gate", j), gate_in.at[:, fcols(y + j)], gate.at[trows(y), :], at(dy=j)),
            send(("up", j), up_in.at[:, fcols(y + j)], up.at[trows(y), :], at(dy=j)),
        )
    gul = (lcopy(gate_in.at[:, fcols(y)], gate.at[trows(y), :]),
           lcopy(up_in.at[:, fcols(y)], up.at[trows(y), :]))

    w1 = {}
    w2 = {}

    def w_x_sends(k):
        blk = w.at[wrows(zl - k, x), :]
        w1[k] = (send(("w1p", k), blk, blk, at(dx=1)), send(("w1m", k), blk, blk, at(dx=3)))

    def w_x_forward(k):
        w1[k][0].wait_recv()
        lo = w.at[wrows(zl - k, x - 1, 0, half_d), :]
        a = send(("w2p", k), lo, lo, at(dx=1))
        w1[k][1].wait_recv()
        hi = w.at[wrows(zl - k, x + 1, half_d, half_d), :]
        b = send(("w2m", k), hi, hi, at(dx=3))
        w2[k] = (a, b)

    g1 = {}
    g2 = {}
    gcs = [gc00]

    def g_y_sends(s):
        blk = gblock(s, 0)
        g1[s] = (send(("g1p", s), blk, blk, at(dy=1)), send(("g1m", s), blk, blk, at(dy=3)))

    def g_core(s, tag, blk):
        gcs.append(send(("gc", s, tag), blk, blk, at(dc=1)))

    def g_y_forward(s):
        g1[s][0].wait_recv()
        lo = gblock(s, -1, 0, half_t)
        a = send(("g2p", s), lo, lo, at(dy=1))
        g_core(s, 1, gblock(s, -1))
        g1[s][1].wait_recv()
        hi = gblock(s, 1, half_t, half_t)
        b = send(("g2m", s), hi, hi, at(dy=3))
        g_core(s, 3, gblock(s, 1))
        g2[s] = (a, b)

    def g_y_last(s):
        g2[s][0].wait_recv()
        g_core(s, 4, gblock(s, 2, 0, half_t))
        g2[s][1].wait_recv()
        g_core(s, 5, gblock(s, 2, half_t, half_t))

    def hidden(yy):
        r0 = trows(yy)

        @pl.loop(0, FB // 128)
        def _(i):
            cs = pl.ds(al(i * 128, 128), 128)
            g = gate[r0, cs].astype(F32)
            u = up[r0, cs].astype(F32)
            h = g * jax.nn.sigmoid(g) * u
            ht[cs, r0] = h.T.astype(BF)

    wl.wait()
    for cp in wy:
        cp.wait_recv()
    own_w = w.at[wrows(zl, x), :]
    wz = {j: send(("wz", j), own_w, own_w, at(dz=j)) for j in (1, 3, 2)}
    w_x_sends(0)
    for cp in gul:
        cp.wait()
    hidden(y)
    gl.wait()
    w_x_forward(0)
    wz[1].wait_recv()
    w_x_sends(1)
    for cp in gu[1]:
        cp.wait_recv()
    g_y_sends(0)
    hidden(y - 1)
    gz.wait_recv()
    g_core(1, 0, gblock(1, 0))
    w_x_forward(1)
    wz[3].wait_recv()
    w_x_sends(3)
    for cp in gu[3]:
        cp.wait_recv()
    g_y_sends(1)
    hidden(y - 3)
    w_x_forward(3)
    wz[2].wait_recv()
    w_x_sends(2)
    for cp in gu[2]:
        cp.wait_recv()
    hidden(y - 2)
    g_y_forward(0)
    w_x_forward(2)
    g_y_forward(1)
    g_y_last(0)
    g_y_last(1)
    for cp in gcs:
        cp.wait_recv()

    nst = len(ids)

    def part(i, dx, h0, n):
        col = al((((zl + 1 + i) % 4) * 4 + (x + dx) % 4) * DB, 128)
        return dot(ht[pl.ds(h0, n), :], go[:, pl.ds(col, DB)])

    def far_copies(i):
        return (
            rcopy(None, far_s.at[i, 0], far_r.at[i, 0], at(dx=1), nst + i),
            rcopy(None, far_s.at[i, 1], far_r.at[i, 1], at(dx=3), nst + 4 + i),
        )

    def near_copies(i):
        return (
            rcopy(None, near_s.at[i, 0], near_r.at[i, 0], at(dx=1), nst + 8 + i),
            rcopy(None, near_s.at[i, 1], near_r.at[i, 1], at(dx=3), nst + 12 + i),
        )

    def far(i):
        cps = far_copies(i)
        for k in range(2):
            far_s[i, k] = part(i, 2, k * half_f, half_f).astype(BF)
            cps[k].start()

    def near(i):
        fcps = far_copies(i)
        cps = near_copies(i)
        for k, dx in ((0, 1), (1, 3)):
            o = 1 - k
            near_s[i, k, pl.ds(o * half_f, half_f), :] = part(i, dx, o * half_f, half_f).astype(BF)
            p = part(i, dx, k * half_f, half_f)
            fcps[k].wait_recv()
            near_s[i, k, pl.ds(k * half_f, half_f), :] = (p + far_r[i, k].astype(F32)).astype(BF)
            cps[k].start()

    def own(i):
        cps = near_copies(i)
        for cp in cps:
            cp.wait_recv()
        for k in range(2):
            r = pl.ds(k * half_f, half_f)
            acc[r, :] = (part(i, 0, k * half_f, half_f) + near_r[i, 0, r, :].astype(F32)
                         + near_r[i, 1, r, :].astype(F32))

    def z_copy(i):
        return rcopy(None, z_s.at[i], z_r.at[i], at(dz=1 + i), nst + 16 + i)

    outs = []

    def out_copies(t):
        j = (2, 1, 3)[t]
        return (
            rcopy(None, ggs.at[t], gg_out.at[:, fcols(y)], at(dy=j), nst + 19 + t),
            rcopy(None, gus.at[t], gu_out.at[:, fcols(y)], at(dy=j), nst + 22 + t),
        )

    def grad_in(t):
        yy = y + (2, 1, 3, 0)[t]
        r0 = al((yy % 4) * T, 16)
        gh[...] = dot(go[pl.ds(r0, T), :], w[...])

        @pl.loop(0, T // 32)
        def _(i):
            r = pl.ds(al(i * 32, 16), 32)
            rr = pl.ds(al(r0 + i * 32, 16), 32)
            g = gate[rr, :].astype(F32)
            u = up[rr, :].astype(F32)
            s = jax.nn.sigmoid(g)
            d = gh[r, :]
            ggs[t, r, :] = (d * u * s * (1.0 + g * (1.0 - s))).astype(BF)
            gus[t, r, :] = (d * (g * s)).astype(BF)

        if t < 3:
            for cp in out_copies(t):
                cp.start()
        else:
            outs.append(lcopy(ggs.at[t], gg_out.at[:, fcols(y)]))
            outs.append(lcopy(gus.at[t], gu_out.at[:, fcols(y)]))

    def own_z(i):
        own(i)
        z_s[i] = acc[...].astype(BF)
        z_copy(i).start()

    far(0)
    far(1)
    near(0)
    for k in (0, 1, 3, 2):
        for cp in w2[k]:
            cp.wait_recv()
    grad_in(0)
    far(2)
    near(1)
    own_z(0)
    grad_in(1)
    far(3)
    near(2)
    own_z(1)
    grad_in(2)
    near(3)
    own_z(2)
    grad_in(3)
    own(3)
    for i in range(3):
        z_copy(i).wait_recv()

    @pl.loop(0, FB // 128)
    def _(i):
        r = pl.ds(al(i * 128, 128), 128)
        tot = acc[r, :] + z_r[0, r, :].astype(F32) + z_r[1, r, :].astype(F32) + z_r[2, r, :].astype(F32)
        fin[:, r] = tot.T.astype(BF)

    def drows(yy):
        return pl.ds(al((yy % 4) * rows_w, 16), rows_w)

    fcp = []
    for t, j in enumerate((2, 1, 3)):
        cp = rcopy(None, fin.at[drows(y + j), :], gd_out.at[:, fcols(y)], at(dy=j), nst + 25 + t)
        cp.start()
        fcp.append(cp)
    outs.append(lcopy(fin.at[drows(y), :], gd_out.at[:, fcols(y)]))

    for cp in sends:
        cp.wait_send()
    for i in range(4):
        for cp in far_copies(i) + near_copies(i):
            cp.wait_send()
    for i in range(3):
        z_copy(i).wait_send()
        for cp in out_copies(i):
            cp.wait()
        fcp[i].wait()
    for cp in outs:
        cp.wait()


def shards(go, gate, up, w):
    T, D = go.shape
    F = gate.shape[1]
    FB, DB = F // 4, w.shape[0] * 4
    vm = lambda *s: pltpu.VMEM(s, BF)
    return pl.pallas_call(
        functools.partial(kernel, T, D, FB, DB),
        out_shape=(
            jax.ShapeDtypeStruct((T, F), BF),
            jax.ShapeDtypeStruct((T, F), BF),
            jax.ShapeDtypeStruct(w.shape, BF),
        ),
        in_specs=[pl.BlockSpec(memory_space=pl.ANY)] * 4,
        out_specs=(pl.BlockSpec(memory_space=pl.ANY),) * 3,
        scratch_shapes=[
            vm(4 * T, 4 * D), vm(16 * DB, FB), vm(4 * T, FB), vm(4 * T, FB), vm(FB, 4 * T),
            pltpu.VMEM((T, FB), F32), vm(4, T, FB), vm(4, T, FB), pltpu.VMEM((FB, DB), F32),
            vm(4, 2, FB // 2, DB), vm(4, 2, FB // 2, DB), vm(4, 2, FB, DB), vm(4, 2, FB, DB),
            vm(3, FB, DB), vm(3, FB, DB), vm(DB, FB),
            pltpu.SemaphoreType.DMA((96,)), pltpu.SemaphoreType.DMA((96,)), pltpu.SemaphoreType.DMA((12,)),
        ],
        compiler_params=pltpu.CompilerParams(
            collective_id=0, has_side_effects=True, vmem_limit_bytes=58 << 20
        ),
        cost_estimate=pl.CostEstimate(
            flops=4 * 4 * T * 4 * D * FB, bytes_accessed=12 * T * F, transcendentals=2 * T * F
        ),
        name="regrouped_backward",
    )(go, gate, up, w)


def solution(mesh):
    fine = Mesh(mesh.devices.reshape(4, 4, 4, 2, 2), AXES)
    spec = P(("zl", "x", "y"), ("zh", "c"))
    return jax.shard_map(
        shards, mesh=fine, in_specs=(spec,) * 4, out_specs=(spec,) * 3, check_vma=False
    )
```

```python
import functools

import jax
import jax.numpy as jnp
from jax import lax
from jax.experimental import pallas as pl
from jax.experimental.pallas import tpu as pltpu
from jax.sharding import Mesh, PartitionSpec as P

AXES = ("zl", "x", "y", "zh", "c")
BF = jnp.bfloat16
F32 = jnp.float32


def dot(a, b):
    return lax.dot_general(a, b, (((1,), (0,)), ((), ())), preferred_element_type=F32)


def kernel(
    T, D, FB, DB,
    go_in, gate_in, up_in, w_in,
    gg_out, gu_out, gd_out,
    go, w, gate, up, ht, gh, ggs, gus, acc,
    far_s, far_r, near_s, near_r, z_s, z_r, fin,
    ssem, rsem, lsem,
):
    zl, x, y, zh, c = (lax.axis_index(a) for a in AXES)
    half_t, half_f, half_d = T // 2, FB // 2, DB // 2
    rows_w = DB // 4

    def al(v, m):
        return pl.multiple_of(v, m)

    def at(dz=0, dx=0, dy=0, dh=0, dc=0):
        return ((zl + dz) % 4, (x + dx) % 4, (y + dy) % 4, (zh + dh) % 2, (c + dc) % 2)

    ids = {}
    sends = []

    def rcopy(src, dst, dev, i, j=None):
        return pltpu.make_async_remote_copy(
            src_ref=src, dst_ref=dst, send_sem=ssem.at[i], recv_sem=rsem.at[i if j is None else j],
            device_id=dev, device_id_type=pl.DeviceIdType.MESH,
        )

    def send(key, src, dst, dev):
        cp = rcopy(src, dst, dev, ids.setdefault(key, len(ids)))
        cp.start()
        sends.append(cp)
        return cp

    nloc = [0]

    def lcopy(src, dst):
        cp = pltpu.make_async_copy(src, dst, lsem.at[nloc[0]])
        nloc[0] += 1
        cp.start()
        return cp

    partners = [at(dy=1), at(dy=2), at(dy=3), at(dx=1), at(dx=3),
                at(dz=1), at(dz=2), at(dz=3), at(dh=1), at(dc=1)]
    bar = pltpu.get_barrier_semaphore()
    for p in partners:
        pl.semaphore_signal(bar, inc=1, device_id=p, device_id_type=pl.DeviceIdType.MESH)
    pl.semaphore_wait(bar, len(partners))

    def fcols(yy):
        return pl.ds(al((yy % 4) * FB, 128), FB)

    def wrows(zz, xx, k=None):
        off, n = (0, DB) if k is None else (k * half_d, half_d)
        return pl.ds(al(((zz % 4) * 4 + xx % 4) * DB + off, 16), n)

    def trows(yy, k=None):
        off, n = (0, T) if k is None else (k * half_t, half_t)
        return pl.ds(al((yy % 4) * T + off, 16), n)

    def quarter(s):
        return 2 * ((zh + s % 2) % 2) + (c + s // 2) % 2

    def gblock(s, dy, k=None):
        return go.at[trows(y + dy, k), pl.ds(al(quarter(s) * D, 128), D)]

    my_w = pl.ds(al(((zl * 4 + x) * 4 + y) * rows_w, 16), rows_w)
    wy = [send(("wy", j), w_in.at[:, fcols(y + j)], w.at[my_w, :], at(dy=j)) for j in (1, 3, 2)]
    wl = lcopy(w_in.at[:, fcols(y)], w.at[my_w, :])
    gul = (lcopy(gate_in.at[:, fcols(y)], gate.at[trows(y), :]),
           lcopy(up_in.at[:, fcols(y)], up.at[trows(y), :]))
    gl = lcopy(go_in, gblock(0, 0))
    gu = {}
    for j in (1, 3, 2):
        gu[j] = (
            send(("gate", j), gate_in.at[:, fcols(y + j)], gate.at[trows(y), :], at(dy=j)),
            send(("up", j), up_in.at[:, fcols(y + j)], up.at[trows(y), :], at(dy=j)),
        )
    gcs = [send(("gc", 0, 0), go_in, gblock(0, 0), at(dc=1))]

    def ring_sends(tag, ref, axis):
        out = {}
        for k in (0, 1):
            out[0, k] = send((tag, "p", k), ref(0, k), ref(0, k), at(**{axis: 1}))
            out[1, k] = send((tag, "m", k), ref(0, 1 - k), ref(0, 1 - k), at(**{axis: 3}))
        return out

    def ring_forward(tag, ref, axis, first):
        first[0, 0].wait_recv()
        a = send((tag, "fp"), ref(-1, 0), ref(-1, 0), at(**{axis: 1}))
        first[1, 0].wait_recv()
        b = send((tag, "fm"), ref(1, 1), ref(1, 1), at(**{axis: 3}))
        return (first[0, 1], first[1, 1], a, b)

    def zsrc(k):
        return (zl, zl + 1 - 2 * (zl % 2), 2 - zl // 2, 3 - 3 * (zl // 2))[k]

    def w_ref(k):
        return lambda dx, h: w.at[wrows(zsrc(k), x + dx, h), :]

    def g_ref(s):
        return lambda dy, h: go.at[trows(y + dy, h), pl.ds(al(quarter(s) * D, 128), D)]

    w1, w2, g1, g2 = {}, {}, {}, {}

    def w_x_sends(k):
        w1[k] = ring_sends(("w", k), w_ref(k), "dx")

    def w_x_forward(k):
        w2[k] = ring_forward(("w", k), w_ref(k), "dx", w1[k])

    def g_y_sends(s):
        g1[s] = ring_sends(("g", s), g_ref(s), "dy")

    def g_y_forward(s):
        g2[s] = ring_forward(("g", s), g_ref(s), "dy", g1[s])

    def g_core(s, tag, blk):
        gcs.append(send(("gc", s, tag), blk, blk, at(dc=1)))

    def g_core_near(s):
        g2[s][0].wait_recv()
        g_core(s, 1, gblock(s, -1))
        g2[s][1].wait_recv()
        g_core(s, 3, gblock(s, 1))

    def g_core_far(s):
        g2[s][2].wait_recv()
        g_core(s, 4, gblock(s, 2, 0))
        g2[s][3].wait_recv()
        g_core(s, 5, gblock(s, 2, 1))

    def hidden(yy):
        r0 = trows(yy)

        @pl.loop(0, FB // 128)
        def _(i):
            cs = pl.ds(al(i * 128, 128), 128)
            g = gate[r0, cs].astype(F32)
            u = up[r0, cs].astype(F32)
            h = g * jax.nn.sigmoid(g) * u
            ht[cs, r0] = h.T.astype(BF)

    wl.wait()
    for cp in wy:
        cp.wait_recv()
    w_x_sends(0)
    zr0 = len(ids)
    for k in range(11):
        ids["wz", k] = len(ids)
    zwhen = []

    def z_w_send(src, dest, i, j, cond):
        blk = w.at[wrows(src, x), :]
        cp = rcopy(blk, blk, (dest, x, y, zh, c), zr0 + i, zr0 + j)

        @pl.when(cond)
        def _():
            cp.start()

        zwhen.append((cond, cp))

    z_w_send(zl, (zl + 1) % 4, 6, 3, zl < 3)
    z_w_send(zl, (zl + 3) % 4, 7, 0, zl > 0)

    def z_w_slot(k):
        src = zsrc(k)
        r = (src - zl + 4) // 4
        step = (src - zl) * (2 * r - 1)
        j = 3 * (1 - r) + step
        blk = w.at[wrows(src, x), :]
        rcopy(blk, blk, at(dz=1), zr0, zr0 + j - 1).wait_recv()
        dest = zl + 1 - 2 * r
        z_w_send(src, (dest + 4) % 4, 7 + k, j % 6, (dest >= 0) & (dest <= 3))

    gz = [send(("gz", 0), go_in.at[pl.ds(0, half_t), :], gblock(0, 0, 0), at(dh=1))]
    gl.wait()
    g_y_sends(0)
    for cp in gul:
        cp.wait()
    hidden(y)
    w_x_forward(0)
    z_w_slot(1)
    w_x_sends(1)
    z_w_slot(2)
    w_x_sends(2)
    gz.append(send(("gz", 1), go_in.at[pl.ds(half_t, half_t), :], gblock(0, 0, 1), at(dh=1)))
    w_x_forward(1)
    for cp in gu[1]:
        cp.wait_recv()
    hidden(y - 1)
    for cp in gu[3]:
        cp.wait_recv()
    hidden(y - 3)
    z_w_slot(3)
    w_x_sends(3)
    w_x_forward(2)
    for cp in gu[2]:
        cp.wait_recv()
    hidden(y - 2)
    g_y_forward(0)
    w_x_forward(3)
    for cp in gz:
        cp.wait_recv()
    g_y_sends(1)
    g_core_near(0)
    g_core(1, 0, gblock(1, 0))
    g_core_far(0)
    for cp in (gcs[i] for i in (0, 1, 2, 4, 5)):
        cp.wait_recv()

    nst = 72
    same = (zh + zl // 2 + 1) % 2
    z1, z2, z3 = zl + 1 - 2 * (zl % 2), (zl + 2) % 4, 3 - zl
    order = (same * z1 + (1 - same) * z2, z3, same * z2 + (1 - same) * z1, zl)

    def part(i, dx, h0, n):
        col = al((order[i] * 4 + (x + dx) % 4) * DB, 128)
        return dot(ht[pl.ds(h0, n), :], go[:, pl.ds(col, DB)])

    def half(k):
        return pl.ds(k * half_f, half_f)

    def far_copies(i):
        return [rcopy(far_s.at[i, k], far_r.at[i, k], at(dx=1 + 2 * k), nst + 2 * i + k) for k in range(2)]

    def near_copies(i):
        return [[rcopy(near_s.at[i, k, half(h)], near_r.at[i, k, half(h)], at(dx=1 + 2 * k),
                       nst + 8 + 4 * i + 2 * k + h) for h in range(2)] for k in range(2)]

    def far(i):
        cps = far_copies(i)
        for k in range(2):
            far_s[i, k] = part(i, 2, k * half_f, half_f).astype(BF)
            cps[k].start()

    def near_own(i):
        cps = near_copies(i)
        for k in range(2):
            h = 1 - k
            near_s[i, k, half(h), :] = part(i, 1 + 2 * k, h * half_f, half_f).astype(BF)
            cps[k][h].start()

    def near_far(i):
        fcps = far_copies(i)
        cps = near_copies(i)
        for k in range(2):
            p = part(i, 1 + 2 * k, k * half_f, half_f)
            fcps[k].wait_recv()
            near_s[i, k, half(k), :] = (p + far_r[i, k].astype(F32)).astype(BF)
            cps[k][k].start()

    def own_part(i, extra=()):
        for h in range(2):
            t = part(i, 0, h * half_f, half_f)
            for e in extra:
                t = t + z_r[e, half(h), :].astype(F32)
            acc[half(h), :] = t

    def near_wait(i, h):
        for k in range(2):
            near_copies(i)[k][h].wait_recv()

    def z_copy(i):
        off = (order[i] - zl) % 4 - 1
        return rcopy(z_s.at[i], z_r.at[off], (order[i], x, y, zh, c), nst + 24 + i, nst + 24 + off)

    def own_z(i):
        own_part(i)
        for h in range(2):
            near_wait(i, h)
            z_s[i, half(h), :] = (acc[half(h), :] + near_r[i, 0, half(h), :].astype(F32)
                                  + near_r[i, 1, half(h), :].astype(F32)).astype(BF)
        z_copy(i).start()

    outs = []

    def out_copies(t):
        j = (2, 1, 3)[t]
        return (
            rcopy(ggs.at[t], gg_out.at[:, fcols(y)], at(dy=j), nst + 27 + t),
            rcopy(gus.at[t], gu_out.at[:, fcols(y)], at(dy=j), nst + 30 + t),
        )

    def grad_in(t):
        yy = y + (2, 1, 3, 0)[t]
        r0 = al((yy % 4) * T, 16)
        gh[...] = dot(go[pl.ds(r0, T), :], w[...])

        @pl.loop(0, T // 32)
        def _(i):
            r = pl.ds(al(i * 32, 16), 32)
            rr = pl.ds(al(r0 + i * 32, 16), 32)
            g = gate[rr, :].astype(F32)
            u = up[rr, :].astype(F32)
            s = jax.nn.sigmoid(g)
            d = gh[r, :]
            ggs[t, r, :] = (d * u * s * (1.0 + g * (1.0 - s))).astype(BF)
            gus[t, r, :] = (d * (g * s)).astype(BF)

        if t < 3:
            for cp in out_copies(t):
                cp.start()
        else:
            outs.append(lcopy(ggs.at[t], gg_out.at[:, fcols(y)]))
            outs.append(lcopy(gus.at[t], gu_out.at[:, fcols(y)]))

    far(0)
    near_own(0)
    g_y_forward(1)
    near_far(0)
    g_core_near(1)
    g_core_far(1)
    for cp in (gcs[i] for i in (3, 6, 7, 8, 9)):
        cp.wait_recv()
    far(1)
    near_own(1)
    for k in range(4):
        for cp in w2[k]:
            cp.wait_recv()
    grad_in(0)
    own_z(0)
    near_far(1)
    far(2)
    near_own(2)
    grad_in(1)
    own_z(1)
    near_far(2)
    grad_in(2)
    far(3)
    near_own(3)
    own_z(2)
    near_far(3)
    grad_in(3)
    for off in range(3):
        rcopy(z_s.at[off], z_r.at[off], at(dz=1 + off), nst + 24 + off).wait_recv()
    own_part(3, (0, 1, 2))
    near_wait(3, 0)
    near_wait(3, 1)

    @pl.loop(0, FB // 128)
    def _(i):
        r = pl.ds(al(i * 128, 128), 128)
        tot = acc[r, :] + near_r[3, 0, r, :].astype(F32) + near_r[3, 1, r, :].astype(F32)
        fin[:, r] = tot.T.astype(BF)

    def drows(yy):
        return pl.ds(al((yy % 4) * rows_w, 16), rows_w)

    fcp = []
    for t, j in enumerate((2, 1, 3)):
        cp = rcopy(fin.at[drows(y + j), :], gd_out.at[:, fcols(y)], at(dy=j), nst + 33 + t)
        cp.start()
        fcp.append(cp)
    outs.append(lcopy(fin.at[drows(y), :], gd_out.at[:, fcols(y)]))

    for cp in sends:
        cp.wait_send()
    for cond, cp in zwhen:
        pl.when(cond)(cp.wait_send)
    for i in range(4):
        for cp in far_copies(i) + sum(near_copies(i), []):
            cp.wait_send()
    for i in range(3):
        z_copy(i).wait_send()
        for cp in out_copies(i):
            cp.wait()
        fcp[i].wait()
    for cp in outs:
        cp.wait()


def shards(go, gate, up, w):
    T, D = go.shape
    F = gate.shape[1]
    FB, DB = F // 4, w.shape[0] * 4
    vm = lambda *s: pltpu.VMEM(s, BF)
    return pl.pallas_call(
        functools.partial(kernel, T, D, FB, DB),
        out_shape=(
            jax.ShapeDtypeStruct((T, F), BF),
            jax.ShapeDtypeStruct((T, F), BF),
            jax.ShapeDtypeStruct(w.shape, BF),
        ),
        in_specs=[pl.BlockSpec(memory_space=pl.ANY)] * 4,
        out_specs=(pl.BlockSpec(memory_space=pl.ANY),) * 3,
        scratch_shapes=[
            vm(4 * T, 4 * D), vm(16 * DB, FB), vm(4 * T, FB), vm(4 * T, FB), vm(FB, 4 * T),
            pltpu.VMEM((T, FB), F32), vm(4, T, FB), vm(4, T, FB), pltpu.VMEM((FB, DB), F32),
            vm(4, 2, FB // 2, DB), vm(4, 2, FB // 2, DB), vm(4, 2, FB, DB), vm(4, 2, FB, DB),
            vm(3, FB, DB), vm(3, FB, DB), vm(DB, FB),
            pltpu.SemaphoreType.DMA((112,)), pltpu.SemaphoreType.DMA((112,)), pltpu.SemaphoreType.DMA((12,)),
        ],
        compiler_params=pltpu.CompilerParams(
            collective_id=0, has_side_effects=True, vmem_limit_bytes=58 << 20
        ),
        cost_estimate=pl.CostEstimate(
            flops=4 * 4 * T * 4 * D * FB, bytes_accessed=12 * T * F, transcendentals=2 * T * F
        ),
        name="regrouped_backward",
    )(go, gate, up, w)


def solution(mesh):
    fine = Mesh(mesh.devices.reshape(4, 4, 4, 2, 2), AXES)
    spec = P(("zl", "x", "y"), ("zh", "c"))
    return jax.shard_map(
        shards, mesh=fine, in_specs=(spec,) * 4, out_specs=(spec,) * 3, check_vma=False
    )
```

```python
import functools

import jax
import jax.numpy as jnp
from jax import lax
from jax.experimental import pallas as pl
from jax.experimental.pallas import tpu as pltpu
from jax.sharding import Mesh, PartitionSpec as P

AXES = ("zl", "x", "y", "zh", "c")
BF = jnp.bfloat16
F32 = jnp.float32


def dot(a, b):
    return lax.dot_general(a, b, (((1,), (0,)), ((), ())), preferred_element_type=F32)


def kernel(
    T, D, FB, DB,
    go_in, gate_in, up_in, w_in,
    gg_out, gu_out, gd_out,
    go, w, gate, up, ht, hs, gh, ghs, ghr, acc,
    far_s, far_r, near_s, near_r, z_s, z_r, fin,
    ssem, rsem, lsem,
):
    zl, x, y, zh, c = (lax.axis_index(a) for a in AXES)
    half_t, half_f, half_d = T // 2, FB // 2, DB // 2
    rows_w = DB // 4

    def al(v, m):
        return pl.multiple_of(v, m)

    def at(dz=0, dx=0, dy=0, dh=0, dc=0):
        return ((zl + dz) % 4, (x + dx) % 4, (y + dy) % 4, (zh + dh) % 2, (c + dc) % 2)

    ids = {}
    sends = []

    def rcopy(src, dst, dev, i, j=None):
        return pltpu.make_async_remote_copy(
            src_ref=src, dst_ref=dst, send_sem=ssem.at[i], recv_sem=rsem.at[i if j is None else j],
            device_id=dev, device_id_type=pl.DeviceIdType.MESH,
        )

    def send(key, src, dst, dev):
        cp = rcopy(src, dst, dev, ids.setdefault(key, len(ids)))
        cp.start()
        sends.append(cp)
        return cp

    nloc = [0]

    def lcopy(src, dst):
        cp = pltpu.make_async_copy(src, dst, lsem.at[nloc[0]])
        nloc[0] += 1
        cp.start()
        return cp

    partners = [at(dy=1), at(dy=2), at(dy=3), at(dx=1), at(dx=3),
                at(dz=1), at(dz=2), at(dz=3), at(dh=1), at(dc=1)]
    bar = pltpu.get_barrier_semaphore()
    for p in partners:
        pl.semaphore_signal(bar, inc=1, device_id=p, device_id_type=pl.DeviceIdType.MESH)
    pl.semaphore_wait(bar, len(partners))

    def fcols(yy):
        return pl.ds(al((yy % 4) * FB, 128), FB)

    def wrows(zz, xx, k=None):
        off, n = (0, DB) if k is None else (k * half_d, half_d)
        return pl.ds(al(((zz % 4) * 4 + xx % 4) * DB + off, 16), n)

    def trows(yy, k=None):
        off, n = (0, T) if k is None else (k * half_t, half_t)
        return pl.ds(al((yy % 4) * T + off, 16), n)

    def quarter(s):
        return 2 * ((zh + s % 2) % 2) + (c + s // 2) % 2

    def gblock(s, dy, k=None):
        return go.at[trows(y + dy, k), pl.ds(al(quarter(s) * D, 128), D)]

    my_w = pl.ds(al(((zl * 4 + x) * 4 + y) * rows_w, 16), rows_w)
    wy = [send(("wy", j), w_in.at[:, fcols(y + j)], w.at[my_w, :], at(dy=j)) for j in (1, 3, 2)]
    wl = lcopy(w_in.at[:, fcols(y)], w.at[my_w, :])
    pieces = {j: (lcopy(gate_in.at[:, fcols(y + j)], gate.at[:, fcols(y + j)]),
                  lcopy(up_in.at[:, fcols(y + j)], up.at[:, fcols(y + j)])) for j in (1, 3, 2, 0)}
    gl = lcopy(go_in, gblock(0, 0))
    gcs = {0: [send(("gc", 0, 0), go_in, gblock(0, 0), at(dc=1))], 1: []}

    def ring_sends(tag, ref, axis):
        out = {}
        for k in (0, 1):
            out[0, k] = send((tag, "p", k), ref(0, k), ref(0, k), at(**{axis: 1}))
            out[1, k] = send((tag, "m", k), ref(0, 1 - k), ref(0, 1 - k), at(**{axis: 3}))
        return out

    def ring_forward(tag, ref, axis, first):
        first[0, 0].wait_recv()
        a = send((tag, "fp"), ref(-1, 0), ref(-1, 0), at(**{axis: 1}))
        first[1, 0].wait_recv()
        b = send((tag, "fm"), ref(1, 1), ref(1, 1), at(**{axis: 3}))
        return (first[0, 1], first[1, 1], a, b)

    def zsrc(k):
        return (zl, zl + 1 - 2 * (zl % 2), 2 - zl // 2, 3 - 3 * (zl // 2))[k]

    def w_ref(k):
        return lambda dx, h: w.at[wrows(zsrc(k), x + dx, h), :]

    def g_ref(s):
        return lambda dy, h: go.at[trows(y + dy, h), pl.ds(al(quarter(s) * D, 128), D)]

    w1, w2, g1, g2 = {}, {}, {}, {}

    def w_x_sends(k):
        w1[k] = ring_sends(("w", k), w_ref(k), "dx")

    def w_x_forward(k):
        w2[k] = ring_forward(("w", k), w_ref(k), "dx", w1[k])

    def g_y_sends(s):
        g1[s] = ring_sends(("g", s), g_ref(s), "dy")

    def g_y_half(s, k):
        for i, sgn in enumerate("pm"):
            g1.setdefault(s, {})[i, k] = send(("g", s, sgn, "h", k), gblock(s, 0, k), gblock(s, 0, k), at(dy=1 + 2 * i))

    def g_y_forward1(s):
        g1[s][0, 0].wait_recv()
        a = send(("g", s, "fp"), gblock(s, -1, 0), gblock(s, -1, 0), at(dy=1))
        g1[s][1, 1].wait_recv()
        b = send(("g", s, "fm"), gblock(s, 1, 1), gblock(s, 1, 1), at(dy=3))
        g2[s] = (g1[s][0, 1], g1[s][1, 0], a, b)

    def g_y_forward(s):
        g2[s] = ring_forward(("g", s), g_ref(s), "dy", g1[s])

    def g_core(s, tag, blk):
        gcs[s].append(send(("gc", s, tag), blk, blk, at(dc=1)))

    def g_core_near(s):
        g2[s][0].wait_recv()
        g_core(s, 1, gblock(s, -1))
        g2[s][1].wait_recv()
        g_core(s, 3, gblock(s, 1))

    def g_core_far(s):
        g2[s][2].wait_recv()
        g_core(s, 4, gblock(s, 2, 0))
        g2[s][3].wait_recv()
        g_core(s, 5, gblock(s, 2, 1))

    def hidden(j, ref):
        for cp in pieces[j]:
            cp.wait()
        c0 = ((y + j) % 4) * FB

        @pl.loop(0, FB // 128)
        def _(i):
            cs = pl.ds(al(c0 + i * 128, 128), 128)
            g = gate[:, cs].astype(F32)
            u = up[:, cs].astype(F32)
            h = g * jax.nn.sigmoid(g) * u
            ref[pl.ds(al(i * 128, 128), 128), :] = h.T.astype(BF)

    hid = []
    tcols = pl.ds(al(y * T, 128), T)
    wl.wait()
    for cp in wy:
        cp.wait_recv()
    w_x_sends(0)
    zr0 = len(ids)
    for k in range(11):
        ids["wz", k] = len(ids)
    zwhen = []

    def z_w_send(src, dest, i, j, cond):
        blk = w.at[wrows(src, x), :]
        cp = rcopy(blk, blk, (dest, x, y, zh, c), zr0 + i, zr0 + j)

        @pl.when(cond)
        def _():
            cp.start()

        zwhen.append((cond, cp))

    z_w_send(zl, (zl + 1) % 4, 6, 3, zl < 3)
    z_w_send(zl, (zl + 3) % 4, 7, 0, zl > 0)

    def z_w_slot(k):
        src = zsrc(k)
        r = (src - zl + 4) // 4
        step = (src - zl) * (2 * r - 1)
        j = 3 * (1 - r) + step
        blk = w.at[wrows(src, x), :]
        rcopy(blk, blk, at(dz=1), zr0, zr0 + j - 1).wait_recv()
        dest = zl + 1 - 2 * r
        z_w_send(src, (dest + 4) % 4, 7 + k, j % 6, (dest >= 0) & (dest <= 3))

    for t, j in enumerate((1, 3, 2)):
        hidden(j, hs.at[t])
        hid.append(send(("hid", j), hs.at[t], ht.at[:, tcols], at(dy=j)))
    gl.wait()
    g_y_sends(0)
    hidden(0, ht.at[:, tcols])
    w_x_forward(0)
    z_w_slot(1)
    w_x_sends(1)
    gz = [send(("gz", 0), go_in.at[pl.ds(0, half_t), :], gblock(0, 0, 0), at(dh=1))]
    z_w_slot(2)
    w_x_sends(2)
    w_x_forward(1)
    z_w_slot(3)
    w_x_sends(3)
    gz.append(send(("gz", 1), go_in.at[pl.ds(half_t, half_t), :], gblock(0, 0, 1), at(dh=1)))
    g_y_forward(0)
    w_x_forward(2)
    g_core_near(0)
    g_core_far(0)
    gz[0].wait_recv()
    g_y_half(1, 0)
    gz[1].wait_recv()
    g_y_half(1, 1)
    g_core(1, 0, gblock(1, 0))
    w_x_forward(3)
    for cp in hid:
        cp.wait_recv()
    for cp in gcs[0]:
        cp.wait_recv()

    nst = 72
    same = (zh + zl // 2 + 1) % 2
    z1, z2, z3 = zl + 1 - 2 * (zl % 2), (zl + 2) % 4, 3 - zl
    order = (same * z1 + (1 - same) * z2, z3, same * z2 + (1 - same) * z1, zl)

    def part(i, dx, h0, n):
        col = al((order[i] * 4 + (x + dx) % 4) * DB, 128)
        return dot(ht[pl.ds(h0, n), :], go[:, pl.ds(col, DB)])

    def half(k):
        return pl.ds(k * half_f, half_f)

    def far_copies(i):
        return [rcopy(far_s.at[i, k], far_r.at[i, k], at(dx=1 + 2 * k), nst + 2 * i + k) for k in range(2)]

    def near_copies(i):
        return [[rcopy(near_s.at[i, k, half(h)], near_r.at[i, k, half(h)], at(dx=1 + 2 * k),
                       nst + 8 + 4 * i + 2 * k + h) for h in range(2)] for k in range(2)]

    def far(i):
        cps = far_copies(i)
        for k in range(2):
            far_s[i, k] = part(i, 2, k * half_f, half_f).astype(BF)
            cps[k].start()

    def near_own(i):
        cps = near_copies(i)
        for k in range(2):
            h = 1 - k
            near_s[i, k, half(h), :] = part(i, 1 + 2 * k, h * half_f, half_f).astype(BF)
            cps[k][h].start()

    def near_far(i):
        fcps = far_copies(i)
        cps = near_copies(i)
        for k in range(2):
            p = part(i, 1 + 2 * k, k * half_f, half_f)
            fcps[k].wait_recv()
            near_s[i, k, half(k), :] = (p + far_r[i, k].astype(F32)).astype(BF)
            cps[k][k].start()

    def own_part(i, extra=()):
        for h in range(2):
            t = part(i, 0, h * half_f, half_f)
            for e in extra:
                t = t + z_r[e, half(h), :].astype(F32)
            acc[half(h), :] = t

    def near_wait(i, h):
        for k in range(2):
            near_copies(i)[k][h].wait_recv()

    def z_copy(i):
        off = (order[i] - zl) % 4 - 1
        return rcopy(z_s.at[i], z_r.at[off], (order[i], x, y, zh, c), nst + 24 + i, nst + 24 + off)

    def own_z(i):
        own_part(i)
        for h in range(2):
            near_wait(i, h)
            z_s[i, half(h), :] = (acc[half(h), :] + near_r[i, 0, half(h), :].astype(F32)
                                  + near_r[i, 1, half(h), :].astype(F32)).astype(BF)
        z_copy(i).start()

    outs = []

    def out_copy(t):
        return rcopy(ghs.at[t], ghr.at[t], at(dy=(2, 1, 3)[t]), nst + 27 + t)

    def grads(yy, ref):
        cs = fcols(yy)

        @pl.loop(0, T // 32)
        def _(i):
            r = pl.ds(al(i * 32, 16), 32)
            g = gate[r, cs].astype(F32)
            u = up[r, cs].astype(F32)
            s = jax.nn.sigmoid(g)
            d = ref[r, :].astype(F32)
            gg_out[r, cs] = (d * u * s * (1.0 + g * (1.0 - s))).astype(BF)
            gu_out[r, cs] = (d * (g * s)).astype(BF)

    def grad_in(t):
        yy = y + (2, 1, 3, 0)[t]
        p = dot(go[pl.ds(al((yy % 4) * T, 16), T), :], w[...])
        if t < 3:
            ghs[t] = p.astype(BF)
            out_copy(t).start()
        else:
            gh[...] = p
            grads(y, gh)

    def grads_from(t):
        out_copy(t).wait_recv()
        grads(y - (2, 1, 3)[t], ghr.at[t])

    far(0)
    near_own(0)
    g_y_forward1(1)
    near_far(0)
    g_core_near(1)
    g_core_far(1)
    for cp in gcs[1]:
        cp.wait_recv()
    far(1)
    near_own(1)
    for k in range(4):
        for cp in w2[k]:
            cp.wait_recv()
    grad_in(0)
    own_z(0)
    near_far(1)
    far(2)
    near_own(2)
    grad_in(1)
    own_z(1)
    near_far(2)
    grad_in(2)
    grads_from(0)
    far(3)
    near_own(3)
    own_z(2)
    near_far(3)
    grad_in(3)
    grads_from(1)
    grads_from(2)
    for off in range(3):
        rcopy(z_s.at[off], z_r.at[off], at(dz=1 + off), nst + 24 + off).wait_recv()
    own_part(3, (0, 1, 2))
    near_wait(3, 0)
    near_wait(3, 1)

    @pl.loop(0, FB // 128)
    def _(i):
        r = pl.ds(al(i * 128, 128), 128)
        tot = acc[r, :] + near_r[3, 0, r, :].astype(F32) + near_r[3, 1, r, :].astype(F32)
        fin[:, r] = tot.T.astype(BF)

    def drows(yy):
        return pl.ds(al((yy % 4) * rows_w, 16), rows_w)

    fcp = []
    for t, j in enumerate((2, 1, 3)):
        cp = rcopy(fin.at[drows(y + j), :], gd_out.at[:, fcols(y)], at(dy=j), nst + 33 + t)
        cp.start()
        fcp.append(cp)
    outs.append(lcopy(fin.at[drows(y), :], gd_out.at[:, fcols(y)]))

    for cp in sends:
        cp.wait_send()
    for cond, cp in zwhen:
        pl.when(cond)(cp.wait_send)
    for i in range(4):
        for cp in far_copies(i) + sum(near_copies(i), []):
            cp.wait_send()
    for i in range(3):
        z_copy(i).wait_send()
        out_copy(i).wait_send()
        fcp[i].wait()
    for cp in outs:
        cp.wait()


def shards(go, gate, up, w):
    T, D = go.shape
    F = gate.shape[1]
    FB, DB = F // 4, w.shape[0] * 4
    vm = lambda *s: pltpu.VMEM(s, BF)
    return pl.pallas_call(
        functools.partial(kernel, T, D, FB, DB),
        out_shape=(
            pltpu.VMEM((T, F), BF),
            pltpu.VMEM((T, F), BF),
            pltpu.VMEM(w.shape, BF),
        ),
        in_specs=[pl.BlockSpec(memory_space=pl.ANY)] * 4,
        out_specs=(pl.BlockSpec(memory_space=pltpu.VMEM),) * 3,
        scratch_shapes=[
            vm(4 * T, 4 * D), vm(16 * DB, FB), vm(T, F), vm(T, F), vm(FB, 4 * T), vm(3, FB, T),
            pltpu.VMEM((T, FB), F32), vm(3, T, FB), vm(3, T, FB), pltpu.VMEM((FB, DB), F32),
            vm(4, 2, FB // 2, DB), vm(4, 2, FB // 2, DB), vm(4, 2, FB, DB), vm(4, 2, FB, DB),
            vm(3, FB, DB), vm(3, FB, DB), vm(DB, FB),
            pltpu.SemaphoreType.DMA((112,)), pltpu.SemaphoreType.DMA((112,)), pltpu.SemaphoreType.DMA((16,)),
        ],
        compiler_params=pltpu.CompilerParams(
            collective_id=0, has_side_effects=True, vmem_limit_bytes=52 << 20
        ),
        cost_estimate=pl.CostEstimate(
            flops=4 * 4 * T * 4 * D * FB, bytes_accessed=12 * T * F, transcendentals=2 * T * F
        ),
        name="regrouped_backward",
    )(go, gate, up, w)


def solution(mesh):
    fine = Mesh(mesh.devices.reshape(4, 4, 4, 2, 2), AXES)
    spec = P(("zl", "x", "y"), ("zh", "c"))
    return jax.shard_map(
        shards, mesh=fine, in_specs=(spec,) * 4, out_specs=(spec,) * 3, check_vma=False
    )
```

```python
import functools

import jax
import jax.numpy as jnp
from jax import lax
from jax.experimental import pallas as pl
from jax.experimental.pallas import tpu as pltpu
from jax.sharding import Mesh, PartitionSpec as P

AXES = ("zl", "x", "y", "zh", "c")
BF = jnp.bfloat16
F32 = jnp.float32


def dot(a, b):
    return lax.dot_general(a, b, (((1,), (0,)), ((), ())), preferred_element_type=F32)


def kernel(
    T, D, FB, DB,
    go_in, gate_in, up_in, w_in,
    gg_out, gu_out, gd_out,
    go, w, gate, up, ht, hs, gh, ghs, ghr, acc,
    far_s, far_r, near_s, near_r, z_s, z_r, fin,
    ssem, rsem, lsem,
):
    zl, x, y, zh, c = (lax.axis_index(a) for a in AXES)
    half_t, half_f, half_d = T // 2, FB // 2, DB // 2
    rows_w = DB // 4

    def al(v, m):
        return pl.multiple_of(v, m)

    def at(dz=0, dx=0, dy=0, dh=0, dc=0):
        return ((zl + dz) % 4, (x + dx) % 4, (y + dy) % 4, (zh + dh) % 2, (c + dc) % 2)

    ids = {}
    sends = []

    def rcopy(src, dst, dev, i, j=None):
        return pltpu.make_async_remote_copy(
            src_ref=src, dst_ref=dst, send_sem=ssem.at[i], recv_sem=rsem.at[i if j is None else j],
            device_id=dev, device_id_type=pl.DeviceIdType.MESH,
        )

    def send(key, src, dst, dev):
        cp = rcopy(src, dst, dev, ids.setdefault(key, len(ids)))
        cp.start()
        sends.append(cp)
        return cp

    nloc = [0]

    def lcopy(src, dst):
        cp = pltpu.make_async_copy(src, dst, lsem.at[nloc[0]])
        nloc[0] += 1
        cp.start()
        return cp

    partners = [at(dy=1), at(dy=2), at(dy=3), at(dx=1), at(dx=3),
                at(dz=1), at(dz=2), at(dz=3), at(dh=1), at(dc=1)]
    bar = pltpu.get_barrier_semaphore()
    for p in partners:
        pl.semaphore_signal(bar, inc=1, device_id=p, device_id_type=pl.DeviceIdType.MESH)

    def fcols(yy):
        return pl.ds(al((yy % 4) * FB, 128), FB)

    def wrows(zz, xx, k=None):
        off, n = (0, DB) if k is None else (k * half_d, half_d)
        return pl.ds(al(((zz % 4) * 4 + xx % 4) * DB + off, 16), n)

    def trows(yy, k=None):
        off, n = (0, T) if k is None else (k * half_t, half_t)
        return pl.ds(al((yy % 4) * T + off, 16), n)

    def quarter(s):
        return 2 * ((zh + s % 2) % 2) + (c + s // 2) % 2

    def gblock(s, dy, k=None):
        return go.at[trows(y + dy, k), pl.ds(al(quarter(s) * D, 128), D)]

    my_w = pl.ds(al(((zl * 4 + x) * 4 + y) * rows_w, 16), rows_w)
    wl = lcopy(w_in.at[:, fcols(y)], w.at[my_w, :])
    pieces = {j: (lcopy(gate_in.at[:, fcols(y + j)], gate.at[:, fcols(y + j)]),
                  lcopy(up_in.at[:, fcols(y + j)], up.at[:, fcols(y + j)])) for j in (1, 3, 2, 0)}
    gl = lcopy(go_in, gblock(0, 0))
    pl.semaphore_wait(bar, len(partners))
    wy = [send(("wy", j), w_in.at[:, fcols(y + j)], w.at[my_w, :], at(dy=j)) for j in (1, 3, 2)]
    gcs = {0: [send(("gc", 0, 0), go_in, gblock(0, 0), at(dc=1))], 1: []}

    def ring_sends(tag, ref, axis):
        out = {}
        for k in (0, 1):
            out[0, k] = send((tag, "p", k), ref(0, k), ref(0, k), at(**{axis: 1}))
            out[1, k] = send((tag, "m", k), ref(0, 1 - k), ref(0, 1 - k), at(**{axis: 3}))
        return out

    def ring_forward(tag, ref, axis, first):
        first[0, 0].wait_recv()
        a = send((tag, "fp"), ref(-1, 0), ref(-1, 0), at(**{axis: 1}))
        first[1, 0].wait_recv()
        b = send((tag, "fm"), ref(1, 1), ref(1, 1), at(**{axis: 3}))
        return (first[0, 1], first[1, 1], a, b)

    def zsrc(k):
        return (zl, zl + 1 - 2 * (zl % 2), 2 - zl // 2, 3 - 3 * (zl // 2))[k]

    def w_ref(k):
        return lambda dx, h: w.at[wrows(zsrc(k), x + dx, h), :]

    def g_ref(s):
        return lambda dy, h: go.at[trows(y + dy, h), pl.ds(al(quarter(s) * D, 128), D)]

    w1, w2, g1, g2 = {}, {}, {}, {}

    def w_x_sends(k):
        w1[k] = ring_sends(("w", k), w_ref(k), "dx")

    def w_x_forward(k):
        w2[k] = ring_forward(("w", k), w_ref(k), "dx", w1[k])

    def g_y_sends(s):
        g1[s] = ring_sends(("g", s), g_ref(s), "dy")

    def g_y_half(s, k):
        for i, sgn in enumerate("pm"):
            g1.setdefault(s, {})[i, k] = send(("g", s, sgn, "h", k), gblock(s, 0, k), gblock(s, 0, k), at(dy=1 + 2 * i))

    def g_y_forward1(s):
        g1[s][0, 0].wait_recv()
        a = send(("g", s, "fp"), gblock(s, -1, 0), gblock(s, -1, 0), at(dy=1))
        g1[s][1, 1].wait_recv()
        b = send(("g", s, "fm"), gblock(s, 1, 1), gblock(s, 1, 1), at(dy=3))
        g2[s] = (g1[s][0, 1], g1[s][1, 0], a, b)

    def g_y_forward(s):
        g2[s] = ring_forward(("g", s), g_ref(s), "dy", g1[s])

    def g_core(s, tag, blk):
        gcs[s].append(send(("gc", s, tag), blk, blk, at(dc=1)))

    def g_core_near(s):
        g2[s][0].wait_recv()
        g_core(s, 1, gblock(s, -1))
        g2[s][1].wait_recv()
        g_core(s, 3, gblock(s, 1))

    def g_core_far(s):
        g2[s][2].wait_recv()
        g_core(s, 4, gblock(s, 2, 0))
        g2[s][3].wait_recv()
        g_core(s, 5, gblock(s, 2, 1))

    def hidden(j, ref):
        for cp in pieces[j]:
            cp.wait()
        c0 = ((y + j) % 4) * FB

        @pl.loop(0, FB // 128)
        def _(i):
            cs = pl.ds(al(c0 + i * 128, 128), 128)
            g = gate[:, cs].astype(F32)
            u = up[:, cs].astype(F32)
            h = g * jax.nn.sigmoid(g) * u
            ref[pl.ds(al(i * 128, 128), 128), :] = h.T.astype(BF)

    hid = []
    tcols = pl.ds(al(y * T, 128), T)
    wl.wait()
    for cp in wy:
        cp.wait_recv()
    w_x_sends(0)
    zr0 = len(ids)
    for k in range(11):
        ids["wz", k] = len(ids)
    zwhen = []

    def z_w_send(src, dest, i, j, cond):
        blk = w.at[wrows(src, x), :]
        cp = rcopy(blk, blk, (dest, x, y, zh, c), zr0 + i, zr0 + j)

        @pl.when(cond)
        def _():
            cp.start()

        zwhen.append((cond, cp))

    z_w_send(zl, (zl + 1) % 4, 6, 3, zl < 3)
    z_w_send(zl, (zl + 3) % 4, 7, 0, zl > 0)

    def z_w_slot(k):
        src = zsrc(k)
        r = (src - zl + 4) // 4
        step = (src - zl) * (2 * r - 1)
        j = 3 * (1 - r) + step
        blk = w.at[wrows(src, x), :]
        rcopy(blk, blk, at(dz=1), zr0, zr0 + j - 1).wait_recv()
        dest = zl + 1 - 2 * r
        z_w_send(src, (dest + 4) % 4, 7 + k, j % 6, (dest >= 0) & (dest <= 3))

    for t, j in enumerate((1, 3, 2)):
        hidden(j, hs.at[t])
        hid.append(send(("hid", j), hs.at[t], ht.at[:, tcols], at(dy=j)))
    gl.wait()
    g_y_sends(0)
    hidden(0, ht.at[:, tcols])
    w_x_forward(0)
    z_w_slot(1)
    w_x_sends(1)
    gz = [send(("gz", 0), go_in.at[pl.ds(0, half_t), :], gblock(0, 0, 0), at(dh=1))]
    z_w_slot(2)
    w_x_sends(2)
    w_x_forward(1)
    z_w_slot(3)
    w_x_sends(3)
    gz.append(send(("gz", 1), go_in.at[pl.ds(half_t, half_t), :], gblock(0, 0, 1), at(dh=1)))
    g_y_forward(0)
    w_x_forward(2)
    g_core_near(0)
    g_core_far(0)
    gz[0].wait_recv()
    g_y_half(1, 0)
    gz[1].wait_recv()
    g_y_half(1, 1)
    g_core(1, 0, gblock(1, 0))
    w_x_forward(3)
    for cp in hid:
        cp.wait_recv()
    for cp in gcs[0]:
        cp.wait_recv()

    nst = 72
    same = (zh + zl // 2 + 1) % 2
    z1, z2, z3 = zl + 1 - 2 * (zl % 2), (zl + 2) % 4, 3 - zl
    order = (same * z1 + (1 - same) * z2, z3, same * z2 + (1 - same) * z1, zl)

    def part(i, dx, h0, n):
        col = al((order[i] * 4 + (x + dx) % 4) * DB, 128)
        return dot(ht[pl.ds(h0, n), :], go[:, pl.ds(col, DB)])

    def half(k):
        return pl.ds(k * half_f, half_f)

    def far_copies(i):
        return [rcopy(far_s.at[i, k], far_r.at[i, k], at(dx=1 + 2 * k), nst + 2 * i + k) for k in range(2)]

    def near_copies(i):
        return [[rcopy(near_s.at[i, k, half(h)], near_r.at[i, k, half(h)], at(dx=1 + 2 * k),
                       nst + 8 + 4 * i + 2 * k + h) for h in range(2)] for k in range(2)]

    def far(i):
        cps = far_copies(i)
        for k in range(2):
            far_s[i, k] = part(i, 2, k * half_f, half_f).astype(BF)
            cps[k].start()

    def near_own(i):
        cps = near_copies(i)
        for k in range(2):
            h = 1 - k
            near_s[i, k, half(h), :] = part(i, 1 + 2 * k, h * half_f, half_f).astype(BF)
            cps[k][h].start()

    def near_far(i):
        fcps = far_copies(i)
        cps = near_copies(i)
        for k in range(2):
            p = part(i, 1 + 2 * k, k * half_f, half_f)
            fcps[k].wait_recv()
            near_s[i, k, half(k), :] = (p + far_r[i, k].astype(F32)).astype(BF)
            cps[k][k].start()

    def own_part(i, extra=()):
        for h in range(2):
            t = part(i, 0, h * half_f, half_f)
            for e in extra:
                t = t + z_r[e, half(h), :].astype(F32)
            acc[half(h), :] = t

    def near_wait(i, h):
        for k in range(2):
            near_copies(i)[k][h].wait_recv()

    def z_copy(i):
        off = (order[i] - zl) % 4 - 1
        return rcopy(z_s.at[i], z_r.at[off], (order[i], x, y, zh, c), nst + 24 + i, nst + 24 + off)

    def own_z(i):
        own_part(i)
        for h in range(2):
            near_wait(i, h)
            z_s[i, half(h), :] = (acc[half(h), :] + near_r[i, 0, half(h), :].astype(F32)
                                  + near_r[i, 1, half(h), :].astype(F32)).astype(BF)
        z_copy(i).start()

    outs = []

    def out_copy(t):
        return rcopy(ghs.at[t], ghr.at[t], at(dy=(2, 1, 3)[t]), nst + 27 + t)

    def grads(yy, ref):
        cs = fcols(yy)

        @pl.loop(0, T // 32)
        def _(i):
            r = pl.ds(al(i * 32, 16), 32)
            g = gate[r, cs].astype(F32)
            u = up[r, cs].astype(F32)
            s = jax.nn.sigmoid(g)
            d = ref[r, :].astype(F32)
            gg_out[r, cs] = (d * u * s * (1.0 + g * (1.0 - s))).astype(BF)
            gu_out[r, cs] = (d * (g * s)).astype(BF)

    def grad_in(t):
        yy = y + (2, 1, 3, 0)[t]
        p = dot(go[pl.ds(al((yy % 4) * T, 16), T), :], w[...])
        if t < 3:
            ghs[t] = p.astype(BF)
            out_copy(t).start()
        else:
            gh[...] = p
            grads(y, gh)

    def grads_from(t):
        out_copy(t).wait_recv()
        grads(y - (2, 1, 3)[t], ghr.at[t])

    far(0)
    near_own(0)
    g_y_forward1(1)
    near_far(0)
    g_core_near(1)
    g_core_far(1)
    for cp in gcs[1]:
        cp.wait_recv()
    far(1)
    near_own(1)
    for k in range(4):
        for cp in w2[k]:
            cp.wait_recv()
    grad_in(0)
    own_z(0)
    near_far(1)
    grad_in(1)
    far(2)
    near_own(2)
    grad_in(2)
    own_z(1)
    near_far(2)
    grad_in(3)
    far(3)
    near_own(3)
    own_z(2)
    near_far(3)
    grads_from(0)
    grads_from(1)
    grads_from(2)
    for off in range(3):
        rcopy(z_s.at[off], z_r.at[off], at(dz=1 + off), nst + 24 + off).wait_recv()
    own_part(3, (0, 1, 2))
    near_wait(3, 0)
    near_wait(3, 1)

    @pl.loop(0, FB // 128)
    def _(i):
        r = pl.ds(al(i * 128, 128), 128)
        tot = acc[r, :] + near_r[3, 0, r, :].astype(F32) + near_r[3, 1, r, :].astype(F32)
        fin[:, r] = tot.T.astype(BF)

    def drows(yy):
        return pl.ds(al((yy % 4) * rows_w, 16), rows_w)

    fcp = []
    for t, j in enumerate((2, 1, 3)):
        cp = rcopy(fin.at[drows(y + j), :], gd_out.at[:, fcols(y)], at(dy=j), nst + 33 + t)
        cp.start()
        fcp.append(cp)
    outs.append(lcopy(fin.at[drows(y), :], gd_out.at[:, fcols(y)]))

    for cp in sends:
        cp.wait_send()
    for cond, cp in zwhen:
        pl.when(cond)(cp.wait_send)
    for i in range(4):
        for cp in far_copies(i) + sum(near_copies(i), []):
            cp.wait_send()
    for i in range(3):
        z_copy(i).wait_send()
        out_copy(i).wait_send()
        fcp[i].wait()
    for cp in outs:
        cp.wait()


def shards(go, gate, up, w):
    T, D = go.shape
    F = gate.shape[1]
    FB, DB = F // 4, w.shape[0] * 4
    vm = lambda *s: pltpu.VMEM(s, BF)
    return pl.pallas_call(
        functools.partial(kernel, T, D, FB, DB),
        out_shape=(
            pltpu.VMEM((T, F), BF),
            pltpu.VMEM((T, F), BF),
            pltpu.VMEM(w.shape, BF),
        ),
        in_specs=[pl.BlockSpec(memory_space=pl.ANY)] * 4,
        out_specs=(pl.BlockSpec(memory_space=pltpu.VMEM),) * 3,
        scratch_shapes=[
            vm(4 * T, 4 * D), vm(16 * DB, FB), vm(T, F), vm(T, F), vm(FB, 4 * T), vm(3, FB, T),
            pltpu.VMEM((T, FB), F32), vm(3, T, FB), vm(3, T, FB), pltpu.VMEM((FB, DB), F32),
            vm(4, 2, FB // 2, DB), vm(4, 2, FB // 2, DB), vm(4, 2, FB, DB), vm(4, 2, FB, DB),
            vm(3, FB, DB), vm(3, FB, DB), vm(DB, FB),
            pltpu.SemaphoreType.DMA((112,)), pltpu.SemaphoreType.DMA((112,)), pltpu.SemaphoreType.DMA((16,)),
        ],
        compiler_params=pltpu.CompilerParams(
            collective_id=0, has_side_effects=True, vmem_limit_bytes=52 << 20
        ),
        cost_estimate=pl.CostEstimate(
            flops=4 * 4 * T * 4 * D * FB, bytes_accessed=12 * T * F, transcendentals=2 * T * F
        ),
        name="regrouped_backward",
    )(go, gate, up, w)


def solution(mesh):
    fine = Mesh(mesh.devices.reshape(4, 4, 4, 2, 2), AXES)
    spec = P(("zl", "x", "y"), ("zh", "c"))
    return jax.shard_map(
        shards, mesh=fine, in_specs=(spec,) * 4, out_specs=(spec,) * 3, check_vma=False
    )
```
